256 devices in a mesh: clip: 32 (over x, z_lo, y), seq: 8 (over z_hi, core).
Axes of the slice: x: 4, y: 4, z: 8 (z_hi: 4, z_lo: 2; z = z_hi * 2 + z_lo), core: 2. Of those that a mesh axis runs over, the one named last changes fastest.
Arguments:
- queries: bfloat16 [49152, 3072], P(('clip', 'seq')), parts along dimension 0, may hold values from -9 to 9
- key_heads: bfloat16 [49152, 3072], P(('clip', 'seq')), parts along dimension 0, may hold values from -9 to 9
- value_heads: bfloat16 [49152, 3072], P(('clip', 'seq')), parts along dimension 0, may hold values from -6 to 6
- query_dot: bfloat16 [49152, 3072], P(('clip', 'seq')), parts along dimension 0, may hold values from -6 to 6
- key_dot: bfloat16 [49152, 3072], P(('clip', 'seq')), parts along dimension 0, may hold values from -6 to 6
- value_dot: bfloat16 [49152, 3072], P(('clip', 'seq')), parts along dimension 0, may hold values from -6 to 6
Outputs:
- attended: bfloat16 [49152, 3072], P(('clip', 'seq')), parts along dimension 0
- attended_dot: bfloat16 [49152, 3072], P(('clip', 'seq')), parts along dimension 0
The draws below stay inside these ranges and needn't reach their ends.
There are 32 independent parts, one for each index of `clip`. The reference program is written for one: setup_inputs(seed, part) draws one part's arguments, and reference() takes and returns one part's arrays. A program takes and returns all parts, laid end to end along the dimension named above; each array names one. Nothing has to cross between parts.
All inputs are finite; a program needn't handle non-finite values.
Results may differ from the reference program's by a relative error of at most 0.039.
Values may be sent and summed in bfloat16 or wider, within the bound.
A program may use at most 128 MiB of HBM per device.

```python
import jax
import jax.numpy as jnp
from jax import lax

H = 24
E = 128
S = 1536


def draw_queries(key, part):
    key = jax.random.fold_in(key, 11)
    field = jnp.clip(1.4 * jax.random.normal(key, (S, H, E), jnp.float32), -8.4, 8.4)
    return field.reshape(S, H * E).astype(jnp.bfloat16)


def draw_key_heads(key, part):
    key = jax.random.fold_in(key, 12)
    field = jnp.clip(1.4 * jax.random.normal(key, (S, H, E), jnp.float32), -8.4, 8.4)
    return field.reshape(S, H * E).astype(jnp.bfloat16)


def level_of(rng, extent, cuts, least, top_value):
    def one(axis_at, shards_of):
        steps = jax.random.uniform(jax.random.fold_in(jax.random.fold_in(rng, 6), axis_at), (shards_of,), jnp.float32, least / len(cuts), top_value / len(cuts))
        return jnp.repeat(jnp.exp(steps), extent[axis_at] // shards_of).reshape((-1,) + (1,) * (len(extent) - axis_at - 1))

    loudness = one(*cuts[0])
    for cut in cuts[1:]:
        loudness = loudness * one(*cut)
    return loudness


def normal_values(rng, shape, width, most, split=(), kind=jnp.bfloat16):
    values = jax.random.normal(rng, shape, jnp.float32) * width
    if len(split) > 0:
        values = level_of(rng, shape, split, -0.22, 0.18) * values
    return jnp.clip(values, min=-most, max=most).astype(kind)


def setup_inputs(seed: int = 0, part: int = 0) -> dict:
    streams_of = jax.random.split(jax.random.key(seed), 7)
    part_keys = jax.random.split(jax.random.fold_in(streams_of[6], part), 7)
    return {
        "queries": draw_queries(jax.random.fold_in(jax.random.fold_in(streams_of[6], part), 71), part),
        "key_heads": draw_key_heads(jax.random.fold_in(jax.random.fold_in(streams_of[6], part), 71), part),
        "value_heads": normal_values(part_keys[2], (S, H * E), 1.0, 6.0, ((0, 8),)),
        "query_dot": normal_values(part_keys[3], (S, H * E), 1.0, 6.0, ((0, 8),)),
        "key_dot": normal_values(part_keys[4], (S, H * E), 1.0, 6.0, ((0, 8),)),
        "value_dot": normal_values(part_keys[5], (S, H * E), 1.0, 6.0, ((0, 8),)),
    }


def attend_block(query_blk, qtan_blk, key_rows, value_rows, key_tan, value_tan, factor):
    scores = jnp.einsum("qhe,khe->hqk", query_blk, key_rows) * factor
    scores_dot = (jnp.einsum("qhe,khe->hqk", qtan_blk, key_rows) + jnp.einsum("qhe,khe->hqk", query_blk, key_tan)) * factor
    highest = jnp.max(scores, axis=2, keepdims=True)
    expd = jnp.exp(scores - highest)
    weights = expd / jnp.sum(expd, axis=2, keepdims=True)
    weights_low = weights.astype(jnp.bfloat16).astype(jnp.float32)
    centre = jnp.sum(weights * scores_dot, axis=2, keepdims=True)
    weights_dot = (weights * (scores_dot - centre)).astype(jnp.bfloat16).astype(jnp.float32)
    attended = jnp.einsum("hqk,khe->qhe", weights_low, value_rows)
    attended_dot = jnp.einsum("hqk,khe->qhe", weights_dot, value_rows) + jnp.einsum("hqk,khe->qhe", weights_low, value_tan)
    return attended.astype(jnp.bfloat16), attended_dot.astype(jnp.bfloat16)


def reference(queries, key_heads, value_heads, query_dot, key_dot, value_dot):
    factor = E ** -0.5
    cubes = [arr.astype(jnp.float32).reshape(S, H, E) for arr in (queries, key_heads, value_heads, query_dot, key_dot, value_dot)]
    block = 512 if S % 512 == 0 else S
    count = S // block

    def one_block(pair):
        return attend_block(pair[0], pair[1], cubes[1], cubes[2], cubes[4], cubes[5], factor)

    result = lax.map(one_block, (cubes[0].reshape(count, block, H, E), cubes[3].reshape(count, block, H, E)))
    return result[0].reshape(S, H * E), result[1].reshape(S, H * E)
```

```python
import functools

import jax
import jax.numpy as jnp
from jax import lax
from jax.experimental import pallas as pl
from jax.experimental.pallas import tpu as pltpu
from jax.sharding import PartitionSpec as P

E = 128
CORES = 2
MESH = pl.DeviceIdType.MESH
LOG2E = 1.4426950408889634
NT = (((1,), (1,)), ((), ()))
NN = (((1,), (0,)), ((), ()))


def attend(query, query_tan, keys, key_tan, values, value_tan):
    factor = E ** (-0.5)
    scores = lax.dot_general(query, keys, NT, preferred_element_type=jnp.float32)
    scores_dot = lax.dot_general(
        jnp.concatenate([query_tan, query], axis=1),
        jnp.concatenate([keys, key_tan], axis=1),
        NT,
        preferred_element_type=jnp.float32,
    )
    highest = jnp.max(scores, axis=1, keepdims=True)
    expd = jnp.exp2((scores - highest) * (factor * LOG2E))
    inverse = 1.0 / jnp.sum(expd, axis=1, keepdims=True)
    centre = jnp.sum(expd * scores_dot, axis=1, keepdims=True) * inverse
    expd_low = expd.astype(jnp.bfloat16)
    expd_dot = (expd * (scores_dot - centre)).astype(jnp.bfloat16)
    both = lax.dot_general(
        expd_low,
        jnp.concatenate([values, value_tan], axis=1),
        NN,
        preferred_element_type=jnp.float32,
    )
    moved = lax.dot_general(expd_dot, values, NN, preferred_element_type=jnp.float32)
    attended = both[:, :E] * inverse
    attended_dot = (moved * factor + both[:, E:]) * inverse
    return attended.astype(jnp.bfloat16), attended_dot.astype(jnp.bfloat16)


def kernel(n, heads, *refs):
    sources, results = refs[:6], refs[6:8]
    held, done = refs[8:10]
    send_in, recv_in, own_in, send_out, recv_out, own_out = refs[10:]
    tokens = sources[0].shape[0]
    chips = n // CORES
    me = lax.axis_index("seq")
    chip, core = me // CORES, lax.rem(me, CORES)

    barrier = pltpu.get_barrier_semaphore()
    for step in range(1, n):
        pl.semaphore_signal(
            barrier, inc=1, device_id={"seq": lax.rem(me + step, n)}, device_id_type=MESH
        )

    def columns(device, head):
        return pl.ds(pl.multiple_of((device * heads + head) * E, E), E)

    def rows(device):
        return pl.ds(pl.multiple_of(device * tokens, tokens), tokens)

    for head in range(heads):
        for i, source in enumerate(sources):
            pltpu.make_async_copy(
                source.at[:, columns(me, head)], held.at[head, i, rows(me)], own_in.at[head]
            ).start()
    pl.semaphore_wait(barrier, n - 1)

    def partner(order):
        over = lax.rem(order, chips)
        over = lax.rem(over + 1, chips)
        side = lax.rem(order // chips + core, CORES)
        return lax.rem(chip + over, chips) * CORES + side

    def send_head(head):
        def to_one(order, carry):
            other = partner(order)

            @pl.when(other != me)
            def _():
                for i, source in enumerate(sources):
                    pltpu.make_async_remote_copy(
                        src_ref=source.at[:, columns(other, head)],
                        dst_ref=held.at[head, i, rows(me)],
                        send_sem=send_in,
                        recv_sem=recv_in.at[head],
                        device_id={"seq": other},
                        device_id_type=MESH,
                    ).start()

            return carry

        lax.fori_loop(0, n, to_one, 0)

    def wait_for(ref, sem):
        pltpu.make_async_copy(ref, ref, sem).wait()

    far = (n - 1) * tokens
    send_head(0)
    send_head(1)

    def one_head(head, carry):
        wait_for(held.at[head, :, pl.ds(0, far)], recv_in.at[head])
        wait_for(held.at[head, :, pl.ds(0, tokens)], own_in.at[head])

        @pl.when(head < heads - 2)
        def _():
            send_head(head + 2)

        def one_chip(step, inner):
            there = lax.rem(chip + 1 + step, chips)
            block = pl.ds(
                pl.multiple_of(there * (CORES * tokens), CORES * tokens), CORES * tokens
            )
            out = attend(
                held[head, 0, block],
                held[head, 3, block],
                held[head, 1],
                held[head, 4],
                held[head, 2],
                held[head, 5],
            )
            for i in range(2):
                done[i, head, block] = out[i]
            for side in range(CORES):
                other = there * CORES + side

                @pl.when(other != me)
                def _():
                    for i in range(2):
                        pltpu.make_async_remote_copy(
                            src_ref=done.at[i, head, rows(other)],
                            dst_ref=results[i].at[:, columns(me, head)],
                            send_sem=send_out,
                            recv_sem=recv_out.at[i],
                            device_id={"seq": other},
                            device_id_type=MESH,
                        ).start()

                @pl.when(other == me)
                def _():
                    for i in range(2):
                        pltpu.make_async_copy(
                            done.at[i, head, rows(me)],
                            results[i].at[:, columns(me, head)],
                            own_out.at[i],
                        ).start()

            return inner

        lax.fori_loop(0, chips, one_chip, 0)
        return carry

    lax.fori_loop(0, heads, one_head, 0)
    wide = (n - 1) * heads * E
    for i in range(2):
        wait_for(results[i].at[:, pl.ds(0, heads * E)], own_out.at[i])
        wait_for(results[i].at[:, pl.ds(0, wide)], recv_out.at[i])
    wait_for(done.at[:, :, pl.ds(0, far)], send_out)
    wait_for(held.at[:, :, pl.ds(0, far)], send_in)


def per_device(n, *arrays):
    tokens, width = arrays[0].shape
    heads = width // E // n
    length = tokens * n
    shape = jax.ShapeDtypeStruct((tokens, width), jnp.bfloat16)
    return pl.pallas_call(
        functools.partial(kernel, n, heads),
        out_shape=(shape, shape),
        in_specs=[pl.BlockSpec(memory_space=pl.ANY)] * 6,
        out_specs=[pl.BlockSpec(memory_space=pl.ANY)] * 2,
        scratch_shapes=[
            pltpu.VMEM((heads, 6, length, E), jnp.bfloat16),
            pltpu.VMEM((2, heads, length, E), jnp.bfloat16),
            pltpu.SemaphoreType.DMA,
            pltpu.SemaphoreType.DMA((heads,)),
            pltpu.SemaphoreType.DMA((heads,)),
            pltpu.SemaphoreType.DMA,
            pltpu.SemaphoreType.DMA((2,)),
            pltpu.SemaphoreType.DMA((2,)),
        ],
        compiler_params=pltpu.CompilerParams(
            collective_id=0, has_side_effects=True, vmem_limit_bytes=56 * 1024 * 1024
        ),
    )(*arrays)


def solution(mesh):
    spec = P(("clip", "seq"), None)
    return jax.shard_map(
        functools.partial(per_device, mesh.shape["seq"]),
        mesh=mesh,
        in_specs=(spec,) * 6,
        out_specs=(spec,) * 2,
        check_vma=False,
    )
```

```python
import functools

import jax
import jax.numpy as jnp
from jax import lax
from jax.experimental import pallas as pl
from jax.experimental.pallas import tpu as pltpu
from jax.sharding import PartitionSpec as P

E = 128
CORES = 2
MESH = pl.DeviceIdType.MESH
LOG2E = 1.4426950408889634
NT = (((1,), (1,)), ((), ()))
NN = (((1,), (0,)), ((), ()))


def attend(query, query_tan, keys, key_tan, values, value_tan):
    factor = E ** (-0.5)
    scores = lax.dot_general(query, keys, NT, preferred_element_type=jnp.float32)
    scores_dot = lax.dot_general(
        jnp.concatenate([query_tan, query], axis=1),
        jnp.concatenate([keys, key_tan], axis=1),
        NT,
        preferred_element_type=jnp.float32,
    )
    highest = jnp.max(scores, axis=1, keepdims=True)
    expd = jnp.exp2((scores - highest) * (factor * LOG2E))
    inverse = 1.0 / jnp.sum(expd, axis=1, keepdims=True)
    centre = jnp.sum(expd * scores_dot, axis=1, keepdims=True) * inverse
    expd_low = expd.astype(jnp.bfloat16)
    expd_dot = (expd * (scores_dot - centre)).astype(jnp.bfloat16)
    both = lax.dot_general(
        expd_low,
        jnp.concatenate([values, value_tan], axis=1),
        NN,
        preferred_element_type=jnp.float32,
    )
    moved = lax.dot_general(expd_dot, values, NN, preferred_element_type=jnp.float32)
    attended = both[:, :E] * inverse
    attended_dot = (moved * factor + both[:, E:]) * inverse
    return attended.astype(jnp.bfloat16), attended_dot.astype(jnp.bfloat16)


def kernel(n, heads, *refs):
    sources, results = refs[:6], refs[6:8]
    held, done = refs[8:10]
    ready, send_in, recv_in, own_in, send_out, recv_out, own_out = refs[10:]
    tokens = sources[0].shape[0]
    chips = n // CORES
    me = lax.axis_index("seq")
    chip, core = me // CORES, lax.rem(me, CORES)
    turned = lax.rem(lax.axis_index("clip") // 4, 2) == 0

    def along(place):
        return jnp.where(turned & (place >= 2), 5 - place, place)

    rank = along(chip) * CORES + (CORES - 1 - core)

    def at_rank(r):
        return along(r // CORES) * CORES + (CORES - 1 - lax.rem(r, CORES))

    def signal(semaphore, device):
        pl.semaphore_signal(
            semaphore, inc=1, device_id={"seq": device}, device_id_type=MESH
        )

    def loop(start, stop, body):
        def step(i, carry):
            body(i)
            return carry

        lax.fori_loop(start, stop, step, 0)

    def columns(device, head):
        return pl.ds(pl.multiple_of((device * heads + head) * E, E), E)

    def rows(device):
        return pl.ds(pl.multiple_of(device * tokens, tokens), tokens)

    def send(head, other):
        for i, source in enumerate(sources):
            pltpu.make_async_remote_copy(
                src_ref=source.at[:, columns(other, head)],
                dst_ref=held.at[head, i, rows(me)],
                send_sem=send_in,
                recv_sem=recv_in.at[head],
                device_id={"seq": other},
                device_id_type=MESH,
            ).start()

    def wait_for(ref, sem):
        pltpu.make_async_copy(ref, ref, sem).wait()

    barrier = pltpu.get_barrier_semaphore()
    loop(rank + 1, n, lambda r: signal(barrier, at_rank(r)))
    pl.when(rank > 0)(lambda: pl.semaphore_wait(barrier, rank))
    loop(0, rank, lambda r: signal(ready.at[me], at_rank(r)))
    loop(0, rank, lambda r: send(0, at_rank(r)))

    def greeted(r):
        pl.semaphore_wait(ready.at[at_rank(r)], 1)
        send(0, at_rank(r))

    loop(rank + 1, n, greeted)

    def own(head):
        for i, source in enumerate(sources):
            pltpu.make_async_copy(
                source.at[:, columns(me, head)], held.at[head, i, rows(me)], own_in.at[head]
            ).start()

    loop(0, heads, own)

    def partner(step):
        over = lax.rem(step // CORES + 1, chips)
        side = 1 - lax.rem(step, CORES)
        return lax.rem(chip + over, chips) * CORES + lax.rem(core + side, CORES)

    def send_head(head):
        loop(0, n - 1, lambda step: send(head, partner(step)))

    def send_out_to(head, other):
        @pl.when(other != me)
        def _():
            for i in range(2):
                pltpu.make_async_remote_copy(
                    src_ref=done.at[i, head, rows(other)],
                    dst_ref=results[i].at[:, columns(me, head)],
                    send_sem=send_out,
                    recv_sem=recv_out.at[i],
                    device_id={"seq": other},
                    device_id_type=MESH,
                ).start()

        @pl.when(other == me)
        def _():
            for i in range(2):
                pltpu.make_async_copy(
                    done.at[i, head, rows(me)],
                    results[i].at[:, columns(me, head)],
                    own_out.at[i],
                ).start()

    far = (n - 1) * tokens
    send_head(1)

    def one_head(head):
        wait_for(held.at[head, :, pl.ds(0, far)], recv_in.at[head])
        wait_for(held.at[head, :, pl.ds(0, tokens)], own_in.at[head])

        @pl.when(head < heads - 2)
        def _():
            send_head(head + 2)

        @pl.when(head > 0)
        def _():
            loop(0, n, lambda step: send_out_to(head - 1, partner(step)))

        def one_device(step):
            other = partner(step)
            block = rows(other)
            out = attend(
                held[head, 0, block],
                held[head, 3, block],
                held[head, 1],
                held[head, 4],
                held[head, 2],
                held[head, 5],
            )
            for i in range(2):
                done[i, head, block] = out[i]
            pl.when(head == heads - 1)(lambda: send_out_to(head, other))

        loop(0, n, one_device)

    loop(0, heads, one_head)
    wide = (n - 1) * heads * E
    for i in range(2):
        wait_for(results[i].at[:, pl.ds(0, heads * E)], own_out.at[i])
        wait_for(results[i].at[:, pl.ds(0, wide)], recv_out.at[i])
    wait_for(done.at[:, :, pl.ds(0, far)], send_out)
    wait_for(held.at[:, :, pl.ds(0, far)], send_in)


def hand_over(one, two, out_one, out_two, sems):
    copies = [
        pltpu.make_async_copy(one, out_one, sems.at[0]),
        pltpu.make_async_copy(two, out_two, sems.at[1]),
    ]
    for copy in copies:
        copy.start()
    for copy in copies:
        copy.wait()


def per_device(n, *arrays):
    tokens, width = arrays[0].shape
    heads = width // E // n
    length = tokens * n
    shape = jax.ShapeDtypeStruct((tokens, width), jnp.bfloat16)
    both = pl.pallas_call(
        functools.partial(kernel, n, heads),
        out_shape=(pltpu.VMEM((tokens, width), jnp.bfloat16),) * 2,
        in_specs=[pl.BlockSpec(memory_space=pltpu.HBM)] * 6,
        out_specs=[pl.BlockSpec(memory_space=pl.ANY)] * 2,
        scratch_shapes=[
            pltpu.VMEM((heads, 6, length, E), jnp.bfloat16),
            pltpu.VMEM((2, heads, length, E), jnp.bfloat16),
            pltpu.SemaphoreType.REGULAR((n,)),
            pltpu.SemaphoreType.DMA,
            pltpu.SemaphoreType.DMA((heads,)),
            pltpu.SemaphoreType.DMA((heads,)),
            pltpu.SemaphoreType.DMA,
            pltpu.SemaphoreType.DMA((2,)),
            pltpu.SemaphoreType.DMA((2,)),
        ],
        compiler_params=pltpu.CompilerParams(
            collective_id=0, has_side_effects=True, vmem_limit_bytes=58 * 1024 * 1024
        ),
    )(*arrays)
    return pl.pallas_call(
        hand_over,
        out_shape=(shape, shape),
        in_specs=[pl.BlockSpec(memory_space=pl.ANY)] * 2,
        out_specs=[pl.BlockSpec(memory_space=pl.ANY)] * 2,
        scratch_shapes=[pltpu.SemaphoreType.DMA((2,))],
    )(*(pltpu.with_memory_space_constraint(one, pltpu.VMEM) for one in both))


def solution(mesh):
    spec = P(("clip", "seq"), None)
    return jax.shard_map(
        functools.partial(per_device, mesh.shape["seq"]),
        mesh=mesh,
        in_specs=(spec,) * 6,
        out_specs=(spec,) * 2,
        check_vma=False,
    )
```

```python
import functools

import jax
import jax.numpy as jnp
from jax import lax
from jax.experimental import pallas as pl
from jax.experimental.pallas import tpu as pltpu
from jax.sharding import PartitionSpec as P

E = 128
CORES = 2
MESH = pl.DeviceIdType.MESH
LOG2E = 1.4426950408889634
NT = (((1,), (1,)), ((), ()))
NN = (((1,), (0,)), ((), ()))


def attend(query, query_tan, keys, key_tan, values, value_tan):
    factor = E ** (-0.5)
    scores = lax.dot_general(query, keys, NT, preferred_element_type=jnp.float32)
    scores_dot = lax.dot_general(
        jnp.concatenate([query_tan, query], axis=1),
        jnp.concatenate([keys, key_tan], axis=1),
        NT,
        preferred_element_type=jnp.float32,
    )
    highest = jnp.max(scores, axis=1, keepdims=True)
    expd = jnp.exp2((scores - highest) * (factor * LOG2E))
    inverse = 1.0 / jnp.sum(expd, axis=1, keepdims=True)
    centre = jnp.sum(expd * scores_dot, axis=1, keepdims=True) * inverse
    expd_low = expd.astype(jnp.bfloat16)
    expd_dot = (expd * (scores_dot - centre)).astype(jnp.bfloat16)
    both = lax.dot_general(
        expd_low,
        jnp.concatenate([values, value_tan], axis=1),
        NN,
        preferred_element_type=jnp.float32,
    )
    moved = lax.dot_general(expd_dot, values, NN, preferred_element_type=jnp.float32)
    attended = both[:, :E] * inverse
    attended_dot = (moved * factor + both[:, E:]) * inverse
    return attended.astype(jnp.bfloat16), attended_dot.astype(jnp.bfloat16)


def kernel(n, heads, *refs):
    sources, results = refs[:6], refs[6:8]
    held, done = refs[8:10]
    ready, send_in, recv_in, own_in, send_out, recv_out, own_out = refs[10:]
    tokens = sources[0].shape[0]
    chips = n // CORES
    me = lax.axis_index("seq")
    chip, core = me // CORES, lax.rem(me, CORES)
    turned = lax.rem(lax.axis_index("clip") // 4, 2) == 0

    def along(place):
        return jnp.where(turned & (place >= 2), 5 - place, place)

    rank = along(chip) * CORES + (CORES - 1 - core)

    def at_rank(r):
        return along(r // CORES) * CORES + (CORES - 1 - lax.rem(r, CORES))

    def signal(semaphore, device):
        pl.semaphore_signal(
            semaphore, inc=1, device_id={"seq": device}, device_id_type=MESH
        )

    def loop(start, stop, body):
        def step(i, carry):
            body(i)
            return carry

        lax.fori_loop(start, stop, step, 0)

    def columns(device, head):
        return pl.ds(pl.multiple_of((device * heads + head) * E, E), E)

    def rows(device):
        return pl.ds(pl.multiple_of(device * tokens, tokens), tokens)

    def send(head, other):
        for i, source in enumerate(sources):
            pltpu.make_async_remote_copy(
                src_ref=source.at[:, columns(other, head)],
                dst_ref=held.at[head, i, rows(me)],
                send_sem=send_in,
                recv_sem=recv_in.at[head],
                device_id={"seq": other},
                device_id_type=MESH,
            ).start()

    def wait_for(ref, sem):
        pltpu.make_async_copy(ref, ref, sem).wait()

    barrier = pltpu.get_barrier_semaphore()
    loop(rank + 1, n, lambda r: signal(barrier, at_rank(r)))
    pl.when(rank > 0)(lambda: pl.semaphore_wait(barrier, rank))
    loop(0, rank, lambda r: signal(ready.at[me], at_rank(r)))
    loop(0, rank, lambda r: send(0, at_rank(r)))

    def greeted(r):
        pl.semaphore_wait(ready.at[at_rank(r)], 1)
        send(0, at_rank(r))

    loop(rank + 1, n, greeted)

    def own(head):
        for i, source in enumerate(sources):
            pltpu.make_async_copy(
                source.at[:, columns(me, head)], held.at[head, i, rows(me)], own_in.at[head]
            ).start()

    loop(0, heads, own)

    def partner(step):
        over = lax.rem(step // CORES + 1, chips)
        side = 1 - lax.rem(step, CORES)
        return lax.rem(chip + over, chips) * CORES + lax.rem(core + side, CORES)

    def send_head(head):
        loop(0, n - 1, lambda step: send(head, partner(step)))

    def send_out_to(head, other):
        @pl.when(other != me)
        def _():
            for i in range(2):
                pltpu.make_async_remote_copy(
                    src_ref=done.at[i, head, rows(other)],
                    dst_ref=results[i].at[:, columns(me, head)],
                    send_sem=send_out,
                    recv_sem=recv_out.at[i],
                    device_id={"seq": other},
                    device_id_type=MESH,
                ).start()

        @pl.when(other == me)
        def _():
            for i in range(2):
                pltpu.make_async_copy(
                    done.at[i, head, rows(me)],
                    results[i].at[:, columns(me, head)],
                    own_out.at[i],
                ).start()

    far = (n - 1) * tokens
    send_head(1)

    def one_head(head):
        wait_for(held.at[head, :, pl.ds(0, far)], recv_in.at[head])
        wait_for(held.at[head, :, pl.ds(0, tokens)], own_in.at[head])

        @pl.when(head < heads - 2)
        def _():
            send_head(head + 2)

        @pl.when(head > 1)
        def _():
            loop(0, n, lambda step: send_out_to(head - 1, partner(step)))

        def one_device(step):
            other = partner(step)
            block = rows(other)
            out = attend(
                held[head, 0, block],
                held[head, 3, block],
                held[head, 1],
                held[head, 4],
                held[head, 2],
                held[head, 5],
            )
            for i in range(2):
                done[i, head, block] = out[i]
            pl.when((head == heads - 1) | (head == 0))(lambda: send_out_to(head, other))

        loop(0, n, one_device)

    loop(0, heads, one_head)
    wide = (n - 1) * heads * E
    for i in range(2):
        wait_for(results[i].at[:, pl.ds(0, heads * E)], own_out.at[i])
        wait_for(results[i].at[:, pl.ds(0, wide)], recv_out.at[i])
    wait_for(done.at[:, :, pl.ds(0, far)], send_out)
    wait_for(held.at[:, :, pl.ds(0, far)], send_in)


def hand_over(one, two, out_one, out_two, sems):
    copies = [
        pltpu.make_async_copy(one, out_one, sems.at[0]),
        pltpu.make_async_copy(two, out_two, sems.at[1]),
    ]
    for copy in copies:
        copy.start()
    for copy in copies:
        copy.wait()


def per_device(n, *arrays):
    tokens, width = arrays[0].shape
    heads = width // E // n
    length = tokens * n
    shape = jax.ShapeDtypeStruct((tokens, width), jnp.bfloat16)
    both = pl.pallas_call(
        functools.partial(kernel, n, heads),
        out_shape=(pltpu.VMEM((tokens, width), jnp.bfloat16),) * 2,
        in_specs=[pl.BlockSpec(memory_space=pltpu.HBM)] * 6,
        out_specs=[pl.BlockSpec(memory_space=pl.ANY)] * 2,
        scratch_shapes=[
            pltpu.VMEM((heads, 6, length, E), jnp.bfloat16),
            pltpu.VMEM((2, heads, length, E), jnp.bfloat16),
            pltpu.SemaphoreType.REGULAR((n,)),
            pltpu.SemaphoreType.DMA,
            pltpu.SemaphoreType.DMA((heads,)),
            pltpu.SemaphoreType.DMA((heads,)),
            pltpu.SemaphoreType.DMA,
            pltpu.SemaphoreType.DMA((2,)),
            pltpu.SemaphoreType.DMA((2,)),
        ],
        compiler_params=pltpu.CompilerParams(
            collective_id=0, has_side_effects=True, vmem_limit_bytes=58 * 1024 * 1024
        ),
    )(*arrays)
    return pl.pallas_call(
        hand_over,
        out_shape=(shape, shape),
        in_specs=[pl.BlockSpec(memory_space=pl.ANY)] * 2,
        out_specs=[pl.BlockSpec(memory_space=pl.ANY)] * 2,
        scratch_shapes=[pltpu.SemaphoreType.DMA((2,))],
    )(*(pltpu.with_memory_space_constraint(one, pltpu.VMEM) for one in both))


def solution(mesh):
    spec = P(("clip", "seq"), None)
    return jax.shard_map(
        functools.partial(per_device, mesh.shape["seq"]),
        mesh=mesh,
        in_specs=(spec,) * 6,
        out_specs=(spec,) * 2,
        check_vma=False,
    )
```
